256 devices in a mesh: dp: 16 (over x, z_hi, core), tensor: 16 (over y, z_lo).
Axes of the slice: x: 4, y: 4, z: 8 (z_hi: 2, z_lo: 4; z = z_hi * 4 + z_lo), core: 2. Of those that a mesh axis runs over, the one named last changes fastest.
Arguments:
- inputs: bfloat16 [16384, 4096], P(('dp', 'tensor')), may hold values from -36 to 36
- out_grad: bfloat16 [16384, 4096], P(('dp', 'tensor')), may hold values from -1.5 to 1.5
- gain: float32 [4096], replicated, may hold values from 0.25 to 1.75
- w_query: bfloat16 [4096, 4096], P(None, 'tensor'), may hold values from -0.09375 to 0.09375
- w_keyval: bfloat16 [2, 4096, 1024], P(None, 'tensor'), may hold values from -0.09375 to 0.09375
- grad_query: bfloat16 [16384, 4096], P('dp', 'tensor'), may hold values from -1.5 to 1.5
- grad_keyval: bfloat16 [2, 16384, 2048], P(None, 'dp', 'tensor'), may hold values from -1.5 to 1.5
Outputs:
- input_grad: float32 [16384, 4096], P(('dp', 'tensor'))
- query_weight_grad: float32 [4096, 4096], P('dp', 'tensor')
- keyval_weight_grad: float32 [2, 4096, 1024], P(None, 'tensor')
The draws below stay inside these ranges and needn't reach their ends.
All inputs are finite; a program needn't handle non-finite values.
Results may differ from the reference program's by a relative error of at most 0.0029.
Values may be sent and summed in bfloat16 or wider, within the bound.
No kernel may reach another device: no remote copies, remote signals or barrier semaphores. Data moves between devices by JAX's collectives and lax.ppermute only.
A program may use at most 128 MiB of HBM per device.

```python
import math
import jax
import jax.numpy as jnp
from jax import lax

D = 4096
QH = 32
KVH = 8
HD = 128
TOK_GROUP = 1024
TOKENS = 16384
COPIES = 2
KV_SLOTS = 16
N_DP = 16


def draw_inputs(key, part):
    key = jax.random.fold_in(key, 11)
    entry_key, row_key, column_key = jax.random.split(key, 3)
    entries = jnp.clip(jax.random.normal(entry_key, (TOKENS, D), jnp.float32), -4.0, 4.0)
    row_scale = jnp.exp(jax.random.uniform(row_key, (TOKENS, 1), jnp.float32, math.log(0.3), math.log(3.0)))
    column_scale = jnp.exp(jax.random.uniform(column_key, (1, D), jnp.float32, math.log(0.3), math.log(3.0)))
    return (entries * row_scale * column_scale).astype(jnp.bfloat16)


def steps_of(rng, shape, pieces, least, top_value):
    level = 1.0
    for position, shards_of in pieces:
        heights = jax.random.uniform(jax.random.fold_in(jax.random.fold_in(rng, 6), position), (shards_of,), jnp.float32, least / len(pieces), top_value / len(pieces))
        level = level * jnp.repeat(jnp.exp(heights), shape[position] // shards_of).reshape((-1,) + (1,) * (len(shape) - 1 - position))
    return level


def gaussian(own_key, dims, scale, bound, cuts=(), kind=jnp.bfloat16):
    level = steps_of(own_key, dims, cuts, -0.22, 0.18) if cuts else 1.0
    values = jax.random.normal(own_key, dims, jnp.float32) * scale * level
    return jnp.minimum(jnp.maximum(values, -bound), bound).astype(kind)


def setup_inputs(seed: int = 0) -> dict:
    key_list = jax.random.split(jax.random.key(seed), 8)
    inputs = draw_inputs(jax.random.fold_in(key_list[7], 71), 0)
    out_grad = gaussian(key_list[1], (TOKENS, D), 0.25, 1.5, ((0, 256),))
    gain = jnp.clip(1.0 + 0.15 * jax.random.normal(key_list[2], (D,), jnp.float32), 0.25, 1.75)
    w_query = gaussian(key_list[3], (D, QH * HD), D ** -0.5, 0.09375, ((1, 16),))
    w_keyval = gaussian(key_list[4], (2, D, KVH * HD), D ** -0.5, 0.09375, ((1, 16),))
    grad_query = gaussian(key_list[5], (TOKENS, QH * HD), 0.25, 1.5, ((0, 16), (1, 16)))
    grad_keyval = gaussian(key_list[6], (2, TOKENS, KV_SLOTS * HD), 0.25, 1.5, ((1, 16), (2, 16)))
    return {"inputs": inputs, "out_grad": out_grad, "gain": gain, "w_query": w_query, "w_keyval": w_keyval, "grad_query": grad_query, "grad_keyval": grad_keyval}


EPSILON = 1e-05

def reference(inputs, out_grad, gain, w_query, w_keyval, grad_query, grad_keyval):
    wide_inputs = inputs.astype(jnp.float32)
    rms_inverse = lax.rsqrt(lax.optimization_barrier(jnp.mean(wide_inputs * wide_inputs, axis=1, keepdims=True)) + EPSILON)
    unit_rows = wide_inputs * rms_inverse
    normed = (unit_rows * gain).astype(jnp.bfloat16)
    keyval_grad = lax.optimization_barrier(jnp.sum(grad_keyval.astype(jnp.float32).reshape(2, TOKENS, KVH, COPIES, HD), axis=3))
    keyval_weight = w_keyval.astype(jnp.float32).reshape(2, D, KVH, HD)
    normed_grad = jnp.dot(grad_query, w_query.T, preferred_element_type=jnp.float32)
    normed_grad = normed_grad + jnp.einsum('pthj,pdhj->td', keyval_grad, keyval_weight, precision=lax.Precision.HIGHEST)
    normed_groups = normed.reshape(N_DP, TOK_GROUP, D)
    query_groups = grad_query.reshape(N_DP, TOK_GROUP, QH * HD)
    keyval_groups = keyval_grad.reshape(2, N_DP, TOK_GROUP, KVH * HD).transpose(1, 0, 2, 3)

    def accumulate(totals, group):
        group_rows, queries, keyvals = group
        part_query = jnp.dot(group_rows.T, queries, preferred_element_type=jnp.float32)
        part_keyval = jnp.einsum('td,ptc->pdc', group_rows.astype(jnp.float32), keyvals, precision=lax.Precision.HIGHEST)
        return ((totals[0] + part_query, totals[1] + part_keyval), None)
    start_totals = (jnp.zeros((D, QH * HD), jnp.float32), jnp.zeros((2, D, KVH * HD), jnp.float32))
    (query_weight_grad, keyval_weight_grad), _ = lax.scan(accumulate, start_totals, (normed_groups, query_groups, keyval_groups))
    scaled = normed_grad * gain
    mean_term = lax.optimization_barrier(jnp.mean(scaled * unit_rows, axis=1, keepdims=True))
    input_grad = out_grad.astype(jnp.float32) + rms_inverse * (scaled - unit_rows * mean_term)
    return (input_grad, query_weight_grad, keyval_weight_grad)
```

```python
import numpy as np
import jax
import jax.numpy as jnp
from jax import lax
from jax.experimental import pallas as pl
from jax.experimental.pallas import tpu as pltpu
from jax.sharding import PartitionSpec as P

EPSILON = 1e-05
BF = jnp.bfloat16
F32 = jnp.float32

INNER = (0, 1, 4, 5)
OUTER = (0, 2, 12, 14)
HEAD_STEP = (0, 1, 6, 7)


def alpha_of(v):
    return (v ^ (v >> 1)) & 1


def ring_place(alpha, beta):
    return alpha ^ (3 * beta)


def place_table():
    rows = []
    for device in range(256):
        dp, t = divmod(device, 16)
        x, c = dp >> 2, dp & 1
        h = (dp >> 1) & 1
        y, z = divmod(t, 4)
        z0, z1 = z & 1, z >> 1
        base = 4 * alpha_of(y) + z0
        outer = 2 * (y >> 1) + z1
        rows.append(
            (
                base,
                t,
                outer,
                x,
                c,
                c ^ z0,
                alpha_of(x) ^ alpha_of(y),
                x >> 1,
                h,
                base ^ OUTER[x],
                (2 * (y ^ (x >> 1)) + z1),
                x & 1,
                (2 * alpha_of(y)) ^ HEAD_STEP[x],
                0,
                0,
                0,
            )
        )
    return np.array(rows, np.int32)


TABLE = place_table()


def exchange(v, axis, flip):
    return lax.ppermute(v, axis, [(i, i ^ flip) for i in range(16)])


def query_turn():
    pairs = []
    for device in range(256):
        dp, t = divmod(device, 16)
        x, h, c = dp >> 2, (dp >> 1) & 1, dp & 1
        y, z = divmod(t, 4)
        x_to = ring_place(alpha_of(y), x >> 1)
        y_to = ring_place(alpha_of(x), y >> 1)
        z_to, c_to = (z & 2) | c, z & 1
        pairs.append((device, (x_to * 4 + h * 2 + c_to) * 16 + y_to * 4 + z_to))
    return pairs


def keyval_turn():
    pairs = []
    for device in range(256):
        dp, t = divmod(device, 16)
        x = dp >> 2
        y, z = divmod(t, 4)
        x_to = 2 * (y >> 1) + (z >> 1)
        y_to = ring_place(alpha_of(y), x >> 1)
        z_to = 2 * (x & 1) + (z & 1)
        pairs.append((device, (x_to * 4 + (dp & 3)) * 16 + y_to * 4 + z_to))
    return pairs


SMEM = pl.BlockSpec(memory_space=pltpu.SMEM)
VMEM = pl.BlockSpec(memory_space=pltpu.VMEM)
ANY = pl.BlockSpec(memory_space=pl.ANY)


def call(kernel, outs, place, args, scratch=(), flops=0, moved=1 << 20, space=VMEM, limit=40):
    return pl.pallas_call(
        kernel,
        out_shape=[jax.ShapeDtypeStruct(s, d) for s, d in outs],
        in_specs=[SMEM] + [space] * len(args),
        out_specs=[space] * len(outs),
        scratch_shapes=list(scratch),
        compiler_params=pltpu.CompilerParams(vmem_limit_bytes=limit << 20),
        cost_estimate=pl.CostEstimate(flops=flops, bytes_accessed=moved, transcendentals=0),
    )(place, *args)


def block(index, size):
    return pl.ds(pl.multiple_of(index * size, size), size)


def norm_kernel(place, x_ref, gain_ref, o0, o1, o2, o3, scr):
    wide = x_ref[...].astype(F32)
    inverse = lax.rsqrt(jnp.mean(wide * wide, axis=1, keepdims=True) + EPSILON)
    scr[...] = ((wide * inverse) * gain_ref[...]).astype(BF)
    base = place[0]
    for k, out in enumerate((o0, o1, o2, o3)):
        for j in range(4):
            out[:, 256 * j : 256 * (j + 1)] = scr[:, block(base ^ (INNER[k] ^ OUTER[j]), 256)]


def weight_pick_kernel(place, wq, wkv, q0, q1, q2, q3, k0, k1, k2, k3, sem):
    copies = []
    for k, out in enumerate((q0, q1, q2, q3)):
        copies.append(pltpu.make_async_copy(wq.at[block(place[9] ^ INNER[k], 256), :], out, sem.at[k]))
    for j, out in enumerate((k0, k1, k2, k3)):
        head = place[10] ^ HEAD_STEP[j]
        copies.append(pltpu.make_async_copy(wkv.at[place[11], :, block(head, 128)], out, sem.at[4 + j]))
    for copy in copies:
        copy.start()
    for copy in copies:
        copy.wait()


def weight_lay_kernel(place, q0, q1, q2, q3, k0, k1, k2, k3, out):
    x, outer = place[3], place[2]
    for i, ref in enumerate((q0, q1, q2, q3)):
        for k in range(4):
            out[x ^ i, :, 256 * k : 256 * (k + 1)] = ref[k]
    for i, ref in enumerate((k0, k1, k2, k3)):
        lanes = pl.ds(pl.multiple_of(1024 + 128 * (x ^ i), 128), 128)
        for j in range(4):
            out[outer ^ j, :, lanes] = ref[j]


def lay_rows(t, j, g, kv, scr):
    for k in range(4):
        rows = block(t ^ (OUTER[j] ^ INNER[k]), 64)
        here = slice(64 * k, 64 * (k + 1))
        for n in range(4):
            scr[here, 256 * n : 256 * (n + 1)] = g[n][rows, :]
        for a in range(2):
            for p in range(2):
                at = 1024 + 128 * (2 * a + p)
                scr[here, at : at + 128] = kv[a][p, rows, :]


def rows_grad_kernel(which, place, g0, g1, g2, g3, kv0, kv1, w, o0, o1, scr):
    t = place[1]
    for j, out in zip(which, (o0, o1)):
        lay_rows(t, j, (g0, g1, g2, g3), (kv0, kv1), scr)
        left = scr[...]
        for d in range(4):
            value = lax.dot_general(left, w[d], (((1,), (1,)), ((), ())), preferred_element_type=F32)
            out[:, 256 * d : 256 * (d + 1)] = value.astype(out.dtype)


def weight_grad_kernel(place, n0, n1, n2, n3, g0, g1, g2, g3, kv0, kv1, q_keep, q_send, kv_keep, kv_send, right):
    t, c, side = place[1], place[4], place[5]
    q_pairs = ((g0, g1), (g2, g3))
    for half, q_out, kv_out in ((1, q_send, kv_send), (0, q_keep, kv_keep)):
        flip = (side ^ half) == 1
        for j in range(4):
            for k in range(4):
                rows = block(t ^ (OUTER[j] ^ INNER[k]), 64)
                here = slice(256 * j + 64 * k, 256 * j + 64 * (k + 1))
                for a in range(2):
                    right[here, 256 * a : 256 * (a + 1)] = jnp.where(flip, q_pairs[a][1][rows, :], q_pairs[a][0][rows, :])
                    kv = (kv0, kv1)[a]
                    right[here, 512 + 128 * a : 512 + 128 * (a + 1)] = kv[c ^ half, rows, :]
        for d in range(4):
            total = None
            for j, n in enumerate((n0, n1, n2, n3)):
                value = lax.dot_general(
                    n[:, 256 * d : 256 * (d + 1)],
                    right[256 * j : 256 * (j + 1), :],
                    (((0,), (0,)), ((), ())),
                    preferred_element_type=F32,
                )
                total = value if total is None else total + value
            rows = slice(256 * d, 256 * (d + 1))
            q_out[0, rows, :] = total[:, :256]
            q_out[1, rows, :] = total[:, 256:512]
            kv_out[rows, :] = total[:, 512:]


def pair_sum_kernel(place, q_keep, q_got, kv_keep, kv_got, o0, o1, o2, o3):
    for i, out in enumerate((o0, o1, o2, o3)):
        a = place[6] ^ (0, 1, 1, 0)[i]
        rows = block(place[7] ^ (i >> 1), 512)
        out[:512, :] = (q_keep[a, rows, :] + q_got[a, rows, :]).astype(out.dtype)
        rows = block(place[3] ^ i, 256)
        out[512:, :] = (kv_keep[rows, :] + kv_got[rows, :]).astype(out.dtype)


def ring_sum_kernel(place, own, r1, r2, r3, q_keep, q_send, kv):
    h = place[8]

    def total(rows):
        return own[rows, :] + r1[rows, :].astype(F32) + r2[rows, :].astype(F32) + r3[rows, :].astype(F32)

    q_keep[...] = total(block(h, 256))
    q_send[...] = total(block(h ^ 1, 256)).astype(BF)
    kv[...] = total(pl.ds(512, 256))


def keyval_lay_kernel(place, a0, a1, a2, a3, b0, b1, b2, b3, out):
    c, head = place[4], place[12]
    for half, refs in ((0, (a0, a1, a2, a3)), (1, (b0, b1, b2, b3))):
        for i, ref in enumerate(refs):
            for a in range(2):
                lanes = block(head ^ (HEAD_STEP[i] ^ (2 * a)), 128)
                out[c ^ half, :, lanes] = ref[:, 128 * a : 128 * (a + 1)]


def input_grad_kernel(place, x_ref, og_ref, gain_ref, p0, p1, p2, p3, out, scaled):
    base = place[0]
    for k, ref in enumerate((p0, p1, p2, p3)):
        for j in range(4):
            lanes = block(base ^ (INNER[k] ^ OUTER[j]), 256)
            scaled[:, lanes] = ref[:, 256 * j : 256 * (j + 1)].astype(F32) * gain_ref[:, lanes]
    wide = x_ref[...].astype(F32)
    inverse = lax.rsqrt(jnp.mean(wide * wide, axis=1, keepdims=True) + EPSILON)
    unit = wide * inverse
    grad = scaled[...]
    mean_term = jnp.mean(grad * unit, axis=1, keepdims=True)
    out[...] = og_ref[...].astype(F32) + inverse * (grad - unit * mean_term)


def shards(inputs, out_grad, gain, w_query, w_keyval, grad_query, grad_keyval):
    device = lax.axis_index("dp") * 16 + lax.axis_index("tensor")
    place = lax.dynamic_index_in_dim(jnp.asarray(TABLE), device, 0, keepdims=False)
    gain_row = gain.reshape(1, 4096)

    kv_pair = exchange(grad_keyval, "tensor", 1)
    g = [grad_query, exchange(grad_query, "tensor", 1), exchange(grad_query, "tensor", 4)]
    kv_own = (grad_keyval.astype(F32) + kv_pair.astype(F32)).astype(BF)
    kv_far = exchange(kv_own, "tensor", 4)
    g.append(exchange(g[1], "tensor", 4))

    pieces = call(norm_kernel, [((64, 1024), BF)] * 4, place, (inputs, gain_row), [pltpu.VMEM((64, 4096), BF)])
    rows = [pieces[0]] + [exchange(pieces[k], "tensor", INNER[k]) for k in (1, 2, 3)]
    n = [jnp.concatenate(rows, axis=0)]
    n.append(exchange(n[0], "tensor", 2))
    n.append(exchange(n[0], "tensor", 12))
    n.append(exchange(n[1], "tensor", 12))

    picked = call(
        weight_pick_kernel,
        [((256, 256), BF)] * 4 + [((256, 128), BF)] * 4,
        place,
        (w_query, w_keyval),
        [pltpu.SemaphoreType.DMA((8,))],
        space=ANY,
    )
    wq = jnp.stack([picked[0]] + [exchange(picked[k], "tensor", INNER[k]) for k in (1, 2, 3)])
    wkv = jnp.stack([picked[4]] + [exchange(picked[4 + j], "tensor", OUTER[j]) for j in (1, 2, 3)])
    wqs = [wq] + [exchange(wq, "dp", 4 * i) for i in (1, 2, 3)]
    wkvs = [wkv] + [exchange(wkv, "dp", 4 * i) for i in (1, 2, 3)]
    (w,) = call(weight_lay_kernel, [((4, 256, 1536), BF)], place, (*wqs, *wkvs))

    def rows_grad(which, kind):
        return call(
            lambda *refs: rows_grad_kernel(which, *refs),
            [((256, 1024), kind)] * 2,
            place,
            (*g, kv_own, kv_far, w),
            [pltpu.VMEM((256, 1536), BF)],
            flops=2 * 512 * 1024 * 1536,
        )

    both, beta = rows_grad((3, 2), BF)
    both_got = exchange(both, "tensor", 12)
    beta_got = exchange(beta, "tensor", 12)
    side, own = rows_grad((1, 0), F32)
    side_got = exchange((side + both_got.astype(F32)).astype(BF), "tensor", 2)
    own = own + beta_got.astype(F32) + side_got.astype(F32)
    parts = [own[64 * k : 64 * (k + 1)] for k in range(4)]
    parts = [parts[0]] + [exchange(parts[k].astype(BF), "tensor", INNER[k]) for k in (1, 2, 3)]
    (input_grad,) = call(
        input_grad_kernel,
        [((64, 4096), F32)],
        place,
        (inputs, out_grad, gain_row, *parts),
        [pltpu.VMEM((64, 4096), F32)],
    )

    q_keep, q_send, kv_keep, kv_send = call(
        weight_grad_kernel,
        [((2, 1024, 256), F32)] * 2 + [((1024, 256), F32)] * 2,
        place,
        (*n, *g, kv_own, kv_far),
        [pltpu.VMEM((1024, 768), BF)],
        flops=2 * 1024 * 1024 * 1536,
    )
    q_got, kv_got = exchange(q_send, "dp", 1), exchange(kv_send, "dp", 1)
    sums = call(
        pair_sum_kernel,
        [((768, 256), F32)] + [((768, 256), BF)] * 3,
        place,
        (q_keep, q_got, kv_keep, kv_got),
    )
    got = [exchange(sums[i], "dp", 4 * i) for i in (1, 2, 3)]
    q_keep, q_send, kv = call(
        ring_sum_kernel,
        [((256, 256), F32), ((256, 256), BF), ((256, 256), F32)],
        place,
        (sums[0], *got),
    )
    q_block = q_keep + exchange(q_send, "dp", 2).astype(F32)
    query_weight_grad = lax.ppermute(q_block, ("dp", "tensor"), query_turn())
    kv = kv + exchange(kv, "dp", 2)
    kv = lax.ppermute(kv, ("dp", "tensor"), keyval_turn())
    near = [kv] + [exchange(kv, "dp", 4 * i) for i in (1, 2, 3)]
    far = [exchange(v, "dp", 1) for v in near]
    (keyval_weight_grad,) = call(keyval_lay_kernel, [((2, 256, 1024), F32)], place, (*near, *far))
    return (input_grad, query_weight_grad, keyval_weight_grad)


def solution(mesh):
    placed = (
        P(("dp", "tensor"), None),
        P(("dp", "tensor"), None),
        P(),
        P(None, "tensor"),
        P(None, "tensor", None),
        P("dp", "tensor"),
        P(None, "dp", "tensor"),
    )
    return jax.shard_map(
        shards,
        mesh=mesh,
        in_specs=placed,
        out_specs=(P(("dp", "tensor"), None), P("dp", "tensor"), P(None, "tensor", None)),
        check_vma=False,
    )
```

```python
import numpy as np
import jax
import jax.numpy as jnp
from jax import lax
from jax.experimental import pallas as pl
from jax.experimental.pallas import tpu as pltpu
from jax.sharding import PartitionSpec as P

EPSILON = 1e-05
BF = jnp.bfloat16
F32 = jnp.float32

INNER = (0, 1, 4, 5)
OUTER = (0, 2, 12, 14)
HEAD_STEP = (0, 1, 6, 7)


def alpha_of(v):
    return (v ^ (v >> 1)) & 1


def ring_place(alpha, beta):
    return alpha ^ (3 * beta)


def place_table():
    rows = []
    for device in range(256):
        dp, t = divmod(device, 16)
        x, c = dp >> 2, dp & 1
        h = (dp >> 1) & 1
        y, z = divmod(t, 4)
        z0, z1 = z & 1, z >> 1
        base = 4 * alpha_of(y) + z0
        outer = 2 * (y >> 1) + z1
        rows.append(
            (
                base,
                t,
                outer,
                x,
                c,
                c ^ z0,
                alpha_of(x) ^ alpha_of(y),
                x >> 1,
                h,
                base ^ OUTER[2 * (x & 1)],
                2 * y + z1,
                x & 1,
                (2 * alpha_of(y)) ^ HEAD_STEP[x],
                0,
                0,
                0,
            )
        )
    return np.array(rows, np.int32)


TABLE = place_table()


def exchange(v, axis, flip):
    return lax.ppermute(v, axis, [(i, i ^ flip) for i in range(16)])


def query_turn(over):
    pairs = []
    for device in range(256):
        dp, t = divmod(device, 16)
        x, h, c = dp >> 2, (dp >> 1) & 1, dp & 1
        y, z = divmod(t, 4)
        x_to = ring_place(alpha_of(y), x >> 1)
        y_to = ring_place(alpha_of(x), y >> 1)
        z_to, c_to = (z & 2) | c, z & 1
        pairs.append((device, (x_to * 4 + (h ^ over) * 2 + c_to) * 16 + y_to * 4 + z_to))
    return pairs


def keyval_turn(over):
    pairs = []
    for device in range(256):
        dp, t = divmod(device, 16)
        x = dp >> 2
        y, z = divmod(t, 4)
        x_to = 2 * (y >> 1) + (z >> 1)
        y_to = ring_place(alpha_of(y), x >> 1)
        z_to = 2 * (x & 1) + (z & 1)
        pairs.append((device, (x_to * 4 + ((dp & 3) ^ (2 * over))) * 16 + y_to * 4 + z_to))
    return pairs


SMEM = pl.BlockSpec(memory_space=pltpu.SMEM)
VMEM = pl.BlockSpec(memory_space=pltpu.VMEM)
ANY = pl.BlockSpec(memory_space=pl.ANY)
HBM = pl.BlockSpec(memory_space=pltpu.HBM)


def call(kernel, outs, place, args, scratch=(), spaces=None, limit=40):
    return pl.pallas_call(
        kernel,
        out_shape=[jax.ShapeDtypeStruct(s, d) for s, d in outs],
        in_specs=[SMEM] + list(spaces or [VMEM] * len(args)),
        out_specs=[VMEM] * len(outs),
        scratch_shapes=list(scratch),
        compiler_params=pltpu.CompilerParams(vmem_limit_bytes=limit << 20),
        cost_estimate=pl.CostEstimate(flops=0, bytes_accessed=1, transcendentals=0),
    )(place, *args)


def block(index, size):
    return pl.ds(pl.multiple_of(index * size, size), size)


def prepare_kernel(place, x_any, gain_any, wq, wkv, *refs):
    inner, k0, k1, k2, x_ref, gain_ref, scr, sem = refs[:4], *refs[4:]
    base, c = place[0], place[4]
    first = [
        pltpu.make_async_copy(x_any, x_ref, sem.at[0]),
        pltpu.make_async_copy(gain_any, gain_ref, sem.at[1]),
    ]
    copies = []
    for k in range(4):
        for m in range(2):
            rows = block(2 * (place[9] ^ (INNER[k] ^ OUTER[m])) + c, 128)
            to = inner[k].at[256 + 128 * m : 384 + 128 * m, :]
            copies.append(pltpu.make_async_copy(wq.at[rows, :], to, sem.at[2 + 2 * k + m]))
    for j, out in enumerate((k0, k1.at[0], k2, k1.at[1])):
        for a in range(2):
            head = block(place[10] ^ (HEAD_STEP[j] ^ (2 * a)), 128)
            to = out.at[:, 128 * a : 128 * (a + 1)]
            copies.append(pltpu.make_async_copy(wkv.at[place[11], block(c, 128), head], to, sem.at[10 + 2 * j + a]))
    for copy in first + copies:
        copy.start()
    for copy in first:
        copy.wait()
    wide = x_ref[...].astype(F32)
    inverse = lax.rsqrt(jnp.mean(wide * wide, axis=1, keepdims=True) + EPSILON)
    scr[...] = ((wide * inverse) * gain_ref[...]).astype(BF)
    for k in range(4):
        for j in range(4):
            inner[k][64 * j : 64 * (j + 1), :] = scr[:, block(base ^ (INNER[k] ^ OUTER[j]), 256)]
    for copy in copies:
        copy.wait()


def gather_rows_kernel(place, m0, m1, m2, m3, gkv, n, gkv_out, sem):
    copy = pltpu.make_async_copy(gkv, gkv_out, sem)
    copy.start()
    for k, ref in enumerate((m0, m1, m2, m3)):
        for j in range(4):
            n[64 * k : 64 * (k + 1), 256 * j : 256 * (j + 1)] = ref[64 * j : 64 * (j + 1), :]
    copy.wait()


def relay_kernel(place, k1, k2, out):
    out[0] = k2[...]
    out[1] = k1[1]


def gather_weights_kernel(place, m0, m1, m2, m3, k0, k1, k23, after, w):
    for k, ref in enumerate((m0, m1, m2, m3)):
        w[k, :256, :] = ref[256:, :]
    for j, piece in enumerate((k0[...], k1[0], k23[0], k23[1])):
        w[j, 256:, :] = piece


def near_kernel(place, own, got, a0, a1, a2, out):
    out[...] = (own[...].astype(F32) + got[...].astype(F32)).astype(BF)


def weight_lay_kernel(place, w0, w1, a0, a1, a2, a3, out):
    outer = place[2]
    for i, ref in enumerate((w0, w1)):
        part = place[11] ^ i
        for k in range(4):
            for m in range(2):
                out[2 * part + m, :, 256 * k : 256 * (k + 1)] = ref[k, 128 * m : 128 * (m + 1), :]
                lanes = pl.ds(pl.multiple_of(1024 + 256 * m + 128 * part, 128), 128)
                out[outer ^ k, :, lanes] = ref[k, 256:, 128 * m : 128 * (m + 1)]


def weight_join_kernel(place, mine, other, out):
    c = place[4]
    for half, ref in ((0, mine), (1, other)):
        for d in range(4):
            out[d, block(c ^ half, 128), :] = ref[d]


def rows_grad_kernel(which, place, g0, g1, g2, g3, kv0, kv1, w, after, o0, o1, scr):
    t = place[1]
    for j, out in zip(which, (o0, o1)):
        for k in range(4):
            rows = block(t ^ (OUTER[j] ^ INNER[k]), 64)
            here = slice(64 * k, 64 * (k + 1))
            for n, g in enumerate((g0, g1, g2, g3)):
                scr[here, 256 * n : 256 * (n + 1)] = g[rows, :]
            for a, kv in enumerate((kv0, kv1)):
                for p in range(2):
                    at = 1024 + 128 * (2 * a + p)
                    scr[here, at : at + 128] = kv[p, rows, :]
        left = scr[...]
        for d in range(4):
            value = lax.dot_general(left, w[d], (((1,), (1,)), ((), ())), preferred_element_type=F32)
            out[:, 256 * d : 256 * (d + 1)] = value.astype(out.dtype)


def rows_product(ns, d, right):
    total = None
    for j, n in enumerate(ns):
        value = lax.dot_general(
            n[:, 256 * d : 256 * (d + 1)],
            right[256 * j : 256 * (j + 1), :],
            (((0,), (0,)), ((), ())),
            preferred_element_type=F32,
        )
        total = value if total is None else total + value
    return total


def keyval_grad_kernel(place, n0, n1, n2, n3, kv0, kv1, after, keep, send, right):
    t, c = place[1], place[4]
    for j in range(4):
        for k in range(4):
            rows = block(t ^ (OUTER[j] ^ INNER[k]), 64)
            here = slice(256 * j + 64 * k, 256 * j + 64 * (k + 1))
            for half in range(2):
                for a, kv in enumerate((kv0, kv1)):
                    at = 256 * half + 128 * a
                    right[here, at : at + 128] = kv[c ^ half, rows, :]
    for d in range(4):
        total = rows_product((n0, n1, n2, n3), d, right)
        keep[256 * d : 256 * (d + 1), :] = total[:, :256]
        send[256 * d : 256 * (d + 1), :] = total[:, 256:]


def query_grad_kernel(place, n0, n1, n2, n3, g0, g1, g2, g3, after, keep, send, right):
    t = place[1]
    flip = place[5] == 1
    for j in range(4):
        for k in range(4):
            rows = block(t ^ (OUTER[j] ^ INNER[k]), 64)
            here = slice(256 * j + 64 * k, 256 * j + 64 * (k + 1))
            for a, (near, far) in enumerate(((g0, g1), (g2, g3))):
                right[here, 256 * a : 256 * (a + 1)] = jnp.where(flip, far[rows, :], near[rows, :])
                right[here, 512 + 256 * a : 768 + 256 * a] = jnp.where(flip, near[rows, :], far[rows, :])
    for d in range(4):
        total = rows_product((n0, n1, n2, n3), d, right)
        for a in range(2):
            keep[a, 256 * d : 256 * (d + 1), :] = total[:, 256 * a : 256 * (a + 1)]
            send[a, 256 * d : 256 * (d + 1), :] = total[:, 512 + 256 * a : 768 + 256 * a]


def keyval_pair_kernel(place, keep, got, o0, o1, o2, o3):
    for i, out in enumerate((o0, o1, o2, o3)):
        rows = block(place[3] ^ i, 256)
        out[...] = (keep[rows, :] + got[rows, :]).astype(out.dtype)


def query_pair_kernel(place, keep, got, after, o0, o1, o2, o3):
    for i, out in enumerate((o0, o1, o2, o3)):
        a = place[6] ^ (0, 1, 1, 0)[i]
        rows = block(place[7] ^ (i >> 1), 512)
        out[...] = (keep[a, rows, :] + got[a, rows, :]).astype(out.dtype)


def query_ring_kernel(place, own, r1, r2, r3, after, q_keep, q_send):
    h = place[8]

    def total(rows):
        return own[rows, :] + r1[rows, :].astype(F32) + r2[rows, :].astype(F32) + r3[rows, :].astype(F32)

    q_keep[...] = total(block(h, 256))
    q_send[...] = total(block(h ^ 1, 256)).astype(BF)


def keyval_ring_kernel(place, own, r1, r2, r3, after, out):
    out[...] = (own[...] + r1[...] + r2[...] + r3[...]).astype(BF)


def keyval_lay_kernel(place, a0, a1, a2, a3, b0, b1, b2, b3, out):
    c, head = place[4], place[12]
    for half, refs in ((0, (a0, a1, a2, a3)), (1, (b0, b1, b2, b3))):
        for i, ref in enumerate(refs):
            for a in range(2):
                lanes = block(head ^ (HEAD_STEP[i] ^ (2 * a)), 128)
                out[c ^ half, :, lanes] = ref[:, 128 * a : 128 * (a + 1)]


def owner_sum_kernel(place, own, beta, side, o0, o1, o2, o3):
    for k, out in enumerate((o0, o1, o2, o3)):
        rows = slice(64 * k, 64 * (k + 1))
        out[...] = (own[rows, :] + beta[rows, :].astype(F32) + side[rows, :].astype(F32)).astype(out.dtype)


def input_grad_kernel(place, x_ref, og_ref, gain_ref, p0, p1, p2, p3, out, scaled):
    base = place[0]
    for k, ref in enumerate((p0, p1, p2, p3)):
        for j in range(4):
            lanes = block(base ^ (INNER[k] ^ OUTER[j]), 256)
            scaled[:, lanes] = ref[:, 256 * j : 256 * (j + 1)].astype(F32) * gain_ref[:, lanes]
    wide = x_ref[...].astype(F32)
    inverse = lax.rsqrt(jnp.mean(wide * wide, axis=1, keepdims=True) + EPSILON)
    unit = wide * inverse
    grad = scaled[...]
    mean_term = jnp.mean(grad * unit, axis=1, keepdims=True)
    out[...] = og_ref[...].astype(F32) + inverse * (grad - unit * mean_term)


def shards(inputs, out_grad, gain, w_query, w_keyval, grad_query, grad_keyval):
    device = lax.axis_index("dp") * 16 + lax.axis_index("tensor")
    place = lax.dynamic_index_in_dim(jnp.asarray(TABLE), device, 0, keepdims=False)
    gain_row = gain.reshape(1, 4096)

    *inner, k0, k1, k2 = call(
        prepare_kernel,
        [((512, 256), BF)] * 4 + [((128, 256), BF), ((2, 128, 256), BF), ((128, 256), BF)],
        place,
        (inputs, gain_row, w_query, w_keyval),
        [
            pltpu.VMEM((64, 4096), BF),
            pltpu.VMEM((1, 4096), F32),
            pltpu.VMEM((64, 4096), BF),
            pltpu.SemaphoreType.DMA((18,)),
        ],
        spaces=[HBM] * 4,
        limit=60,
    )
    inner = [inner[0]] + [exchange(inner[k], "tensor", INNER[k]) for k in (1, 2, 3)]
    k1 = exchange(k1, "tensor", 2)
    g1, g2 = exchange(grad_query, "tensor", 1), exchange(grad_query, "tensor", 4)
    g = (grad_query, g1, g2, exchange(g1, "tensor", 4))
    n0, gkv = call(
        gather_rows_kernel,
        [((256, 1024), BF), ((2, 1024, 128), BF)],
        place,
        (*inner, grad_keyval),
        [pltpu.SemaphoreType.DMA],
        spaces=[VMEM] * 4 + [HBM],
    )
    (k23,) = call(relay_kernel, [((2, 128, 256), BF)], place, (k1, k2))
    k23 = exchange(k23, "tensor", 12)
    n1 = exchange(n0, "tensor", 2)
    n = (n0, n1, exchange(n0, "tensor", 12), exchange(n1, "tensor", 12))
    (w0,) = call(
        gather_weights_kernel,
        [((4, 384, 256), BF)],
        place,
        (*inner, k0, k1, k23, g1),
        spaces=[VMEM] * 7 + [ANY],

    )
    (kv_own,) = call(
        near_kernel,
        [((2, 1024, 128), BF)],
        place,
        (gkv, exchange(gkv, "tensor", 1), w0, n1, n[2]),
        spaces=[VMEM] * 2 + [ANY] * 3,
    )
    kv_far = exchange(kv_own, "tensor", 4)
    (half,) = call(
        weight_lay_kernel,
        [((4, 128, 1536), BF)],
        place,
        (w0, exchange(w0, "dp", 4), kv_far, g[3], g2, n[3]),
        spaces=[VMEM] * 2 + [ANY] * 4,
    )
    (w,) = call(weight_join_kernel, [((4, 256, 1536), BF)], place, (half, exchange(half, "dp", 1)))

    kv_keep, kv_send = call(
        keyval_grad_kernel,
        [((1024, 256), F32)] * 2,
        place,
        (*n, kv_own, kv_far, half),
        [pltpu.VMEM((1024, 512), BF)],
        spaces=[VMEM] * 6 + [ANY],
    )

    kv = call(
        keyval_pair_kernel,
        [((256, 256), F32)] * 4,
        place,
        (kv_keep, exchange(kv_send, "dp", 1)),
    )

    def rows_grad(which, kind, after):
        return call(
            lambda *refs: rows_grad_kernel(which, *refs),
            [((256, 1024), kind)] * 2,
            place,
            (*g, kv_own, kv_far, w, after),
            [pltpu.VMEM((256, 1536), BF)],
            spaces=[VMEM] * 7 + [ANY],
        )

    both, beta = rows_grad((3, 2), BF, kv[0])
    both_got = exchange(both, "tensor", 12)
    beta_got = exchange(beta, "tensor", 12)
    q_keep, q_send = call(
        query_grad_kernel,
        [((2, 1024, 256), F32)] * 2,
        place,
        (*n, *g, both),
        [pltpu.VMEM((1024, 1024), BF)],
        spaces=[VMEM] * 8 + [ANY],
    )
    q_got = exchange(q_send, "dp", 1)
    q = call(
        query_pair_kernel,
        [((512, 256), F32)] + [((512, 256), BF)] * 3,
        place,
        (q_keep, q_got, kv[0]),
        spaces=[VMEM] * 2 + [ANY],
    )
    side, own = rows_grad((1, 0), F32, q[0])
    side = (side + both_got.astype(F32)).astype(BF)
    side_got = exchange(side, "tensor", 2)

    everywhere = ("dp", "tensor")
    (kv,) = call(
        keyval_ring_kernel,
        [((256, 256), BF)],
        place,
        (kv[0], *(exchange(kv[i], "dp", 4 * i) for i in (1, 2, 3)), side),
        spaces=[VMEM] * 4 + [ANY],
    )
    kv = [lax.ppermute(kv, everywhere, keyval_turn(over)).astype(F32) for over in (0, 1)]
    kv = kv[0] + kv[1]
    near = [kv] + [exchange(kv, "dp", 4 * i) for i in (1, 2, 3)]
    far = [exchange(v, "dp", 1) for v in near]
    (keyval_weight_grad,) = call(keyval_lay_kernel, [((2, 256, 1024), F32)], place, (*near, *far))

    parts = call(
        owner_sum_kernel, [((64, 1024), F32)] + [((64, 1024), BF)] * 3, place, (own, beta_got, side_got)
    )
    parts = [parts[0]] + [exchange(parts[k], "tensor", INNER[k]) for k in (1, 2, 3)]
    (input_grad,) = call(
        input_grad_kernel,
        [((64, 4096), F32)],
        place,
        (inputs, out_grad, gain_row, *parts),
        [pltpu.VMEM((64, 4096), F32)],
    )

    q_keep, q_send = call(
        query_ring_kernel,
        [((256, 256), F32), ((256, 256), BF)],
        place,
        (q[0], *(exchange(q[i], "dp", 4 * i) for i in (1, 2, 3)), parts[0]),
        spaces=[VMEM] * 4 + [ANY],
    )
    query_weight_grad = lax.ppermute(q_keep, everywhere, query_turn(0)) + lax.ppermute(
        q_send, everywhere, query_turn(1)
    ).astype(F32)
    return (input_grad, query_weight_grad, keyval_weight_grad)


def solution(mesh):
    placed = (
        P(("dp", "tensor"), None),
        P(("dp", "tensor"), None),
        P(),
        P(None, "tensor"),
        P(None, "tensor", None),
        P("dp", "tensor"),
        P(None, "dp", "tensor"),
    )
    return jax.shard_map(
        shards,
        mesh=mesh,
        in_specs=placed,
        out_specs=(P(("dp", "tensor"), None), P("dp", "tensor"), P(None, "tensor", None)),
        check_vma=False,
    )
```

```python
import numpy as np
import jax
import jax.numpy as jnp
from jax import lax
from jax.experimental import pallas as pl
from jax.experimental.pallas import tpu as pltpu
from jax.sharding import PartitionSpec as P

EPSILON = 1e-05
BF = jnp.bfloat16
F32 = jnp.float32

INNER = (0, 1, 4, 5)
OUTER = (0, 2, 12, 14)
HEAD_STEP = (0, 1, 6, 7)


def alpha_of(v):
    return (v ^ (v >> 1)) & 1


def ring_place(alpha, beta):
    return alpha ^ (3 * beta)


def place_table():
    rows = []
    for device in range(256):
        dp, t = divmod(device, 16)
        x, c = dp >> 2, dp & 1
        h = (dp >> 1) & 1
        y, z = divmod(t, 4)
        z0, z1 = z & 1, z >> 1
        base = 4 * alpha_of(y) + z0
        outer = 2 * (y >> 1) + z1
        rows.append(
            (
                base,
                t,
                outer,
                x,
                c,
                c ^ z0,
                alpha_of(x) ^ alpha_of(y),
                x >> 1,
                h,
                base ^ OUTER[2 * (x & 1)],
                2 * y + z1,
                x & 1,
                (2 * alpha_of(y)) ^ HEAD_STEP[x],
                0,
                0,
                0,
            )
        )
    return np.array(rows, np.int32)


TABLE = place_table()


def exchange(v, axis, flip):
    return lax.ppermute(v, axis, [(i, i ^ flip) for i in range(16)])


def query_turn(over):
    pairs = []
    for device in range(256):
        dp, t = divmod(device, 16)
        x, h, c = dp >> 2, (dp >> 1) & 1, dp & 1
        y, z = divmod(t, 4)
        x_to = ring_place(alpha_of(y), x >> 1)
        y_to = ring_place(alpha_of(x), y >> 1)
        z_to, c_to = (z & 2) | c, z & 1
        pairs.append((device, (x_to * 4 + (h ^ over) * 2 + c_to) * 16 + y_to * 4 + z_to))
    return pairs


def keyval_turn(over):
    pairs = []
    for device in range(256):
        dp, t = divmod(device, 16)
        x = dp >> 2
        y, z = divmod(t, 4)
        x_to = 2 * (y >> 1) + (z >> 1)
        y_to = ring_place(alpha_of(y), x >> 1)
        z_to = 2 * (x & 1) + (z & 1)
        pairs.append((device, (x_to * 4 + ((dp & 3) ^ (2 * over))) * 16 + y_to * 4 + z_to))
    return pairs


SMEM = pl.BlockSpec(memory_space=pltpu.SMEM)
VMEM = pl.BlockSpec(memory_space=pltpu.VMEM)
ANY = pl.BlockSpec(memory_space=pl.ANY)
HBM = pl.BlockSpec(memory_space=pltpu.HBM)


def call(kernel, outs, place, args, scratch=(), spaces=None, limit=40, cost=0):
    return pl.pallas_call(
        kernel,
        out_shape=[jax.ShapeDtypeStruct(s, d) for s, d in outs],
        in_specs=[SMEM] + list(spaces or [VMEM] * len(args)),
        out_specs=[VMEM] * len(outs),
        scratch_shapes=list(scratch),
        compiler_params=pltpu.CompilerParams(vmem_limit_bytes=limit << 20),
        cost_estimate=pl.CostEstimate(flops=cost, bytes_accessed=1, transcendentals=0),
    )(place, *args)


def block(index, size):
    return pl.ds(pl.multiple_of(index * size, size), size)


def prepare_kernel(place, x_any, gain_any, wq, wkv, *refs):
    inner, k0, k1, k2, x_ref, gain_ref, scr, sem = refs[:4], *refs[4:]
    base, c = place[0], place[4]
    first = [
        pltpu.make_async_copy(x_any, x_ref, sem.at[0]),
        pltpu.make_async_copy(gain_any, gain_ref, sem.at[1]),
    ]
    copies = []
    for k in range(4):
        for m in range(2):
            rows = block(2 * (place[9] ^ (INNER[k] ^ OUTER[m])) + c, 128)
            to = inner[k].at[256 + 128 * m : 384 + 128 * m, :]
            copies.append(pltpu.make_async_copy(wq.at[rows, :], to, sem.at[2 + 2 * k + m]))
    for j, out in enumerate((k0, k1.at[0], k2, k1.at[1])):
        for a in range(2):
            head = block(place[10] ^ (HEAD_STEP[j] ^ (2 * a)), 128)
            to = out.at[:, 128 * a : 128 * (a + 1)]
            copies.append(pltpu.make_async_copy(wkv.at[place[11], block(c, 128), head], to, sem.at[10 + 2 * j + a]))
    for copy in first + copies:
        copy.start()
    for copy in first:
        copy.wait()
    wide = x_ref[...].astype(F32)
    inverse = lax.rsqrt(jnp.mean(wide * wide, axis=1, keepdims=True) + EPSILON)
    scr[...] = ((wide * inverse) * gain_ref[...]).astype(BF)
    for k in range(4):
        for j in range(4):
            inner[k][64 * j : 64 * (j + 1), :] = scr[:, block(base ^ (INNER[k] ^ OUTER[j]), 256)]
    for copy in copies:
        copy.wait()


def gather_rows_kernel(place, m0, m1, m2, m3, k1, k2, gkv, n, k23, gkv_out, sem):
    copy = pltpu.make_async_copy(gkv, gkv_out, sem)
    copy.start()
    for k, ref in enumerate((m0, m1, m2, m3)):
        for j in range(4):
            n[64 * k : 64 * (k + 1), 256 * j : 256 * (j + 1)] = ref[64 * j : 64 * (j + 1), :]
    k23[0] = k2[...]
    k23[1] = k1[1]
    copy.wait()


def gather_weights_kernel(place, m0, m1, m2, m3, k0, k1, k23, after, w):
    for k, ref in enumerate((m0, m1, m2, m3)):
        w[k, :256, :] = ref[256:, :]
    for j, piece in enumerate((k0[...], k1[0], k23[0], k23[1])):
        w[j, 256:, :] = piece


def near_kernel(place, own, got, a0, a1, a2, out):
    out[...] = (own[...].astype(F32) + got[...].astype(F32)).astype(BF)


def weight_lay_kernel(place, w0, w1, a0, a1, a2, out):
    outer = place[2]
    for i, ref in enumerate((w0, w1)):
        part = place[11] ^ i
        for k in range(4):
            for m in range(2):
                out[2 * part + m, :, 256 * k : 256 * (k + 1)] = ref[k, 128 * m : 128 * (m + 1), :]
                lanes = pl.ds(pl.multiple_of(1024 + 256 * m + 128 * part, 128), 128)
                out[outer ^ k, :, lanes] = ref[k, 256:, 128 * m : 128 * (m + 1)]


def weight_join_kernel(place, mine, other, out):
    c = place[4]
    for half, ref in ((0, mine), (1, other)):
        for d in range(4):
            out[d, block(c ^ half, 128), :] = ref[d]


def rows_grad_kernel(which, place, g0, g1, g2, g3, kv0, kv1, w, after, o0, o1, scr):
    t = place[1]
    for j, out in zip(which, (o0, o1)):
        for k in range(4):
            rows = block(t ^ (OUTER[j] ^ INNER[k]), 64)
            here = slice(64 * k, 64 * (k + 1))
            for n, g in enumerate((g0, g1, g2, g3)):
                scr[here, 256 * n : 256 * (n + 1)] = g[rows, :]
            for a, kv in enumerate((kv0, kv1)):
                for p in range(2):
                    at = 1024 + 128 * (2 * a + p)
                    scr[here, at : at + 128] = kv[p, rows, :]
        left = scr[...]
        for d in range(4):
            value = lax.dot_general(left, w[d], (((1,), (1,)), ((), ())), preferred_element_type=F32)
            out[:, 256 * d : 256 * (d + 1)] = value.astype(out.dtype)


def rows_product(ns, d, right):
    total = None
    for j, n in enumerate(ns):
        value = lax.dot_general(
            n[:, 256 * d : 256 * (d + 1)],
            right[256 * j : 256 * (j + 1), :],
            (((0,), (0,)), ((), ())),
            preferred_element_type=F32,
        )
        total = value if total is None else total + value
    return total


def keyval_grad_kernel(place, n0, n1, n2, n3, kv0, kv1, after, keep, send, right):
    t, c = place[1], place[4]
    for j in range(4):
        for k in range(4):
            rows = block(t ^ (OUTER[j] ^ INNER[k]), 64)
            here = slice(256 * j + 64 * k, 256 * j + 64 * (k + 1))
            for half in range(2):
                for a, kv in enumerate((kv0, kv1)):
                    at = 256 * half + 128 * a
                    right[here, at : at + 128] = kv[c ^ half, rows, :]
    for d in range(4):
        total = rows_product((n0, n1, n2, n3), d, right)
        keep[256 * d : 256 * (d + 1), :] = total[:, :256]
        send[256 * d : 256 * (d + 1), :] = total[:, 256:]


def query_grad_kernel(place, n0, n1, n2, n3, g0, g1, g2, g3, after, keep, send, right):
    t = place[1]
    flip = place[5] == 1
    for j in range(4):
        for k in range(4):
            rows = block(t ^ (OUTER[j] ^ INNER[k]), 64)
            here = slice(256 * j + 64 * k, 256 * j + 64 * (k + 1))
            for a, (near, far) in enumerate(((g0, g1), (g2, g3))):
                right[here, 256 * a : 256 * (a + 1)] = jnp.where(flip, far[rows, :], near[rows, :])
                right[here, 512 + 256 * a : 768 + 256 * a] = jnp.where(flip, near[rows, :], far[rows, :])
    for d in range(4):
        total = rows_product((n0, n1, n2, n3), d, right)
        for a in range(2):
            keep[a, 256 * d : 256 * (d + 1), :] = total[:, 256 * a : 256 * (a + 1)]
            send[a, 256 * d : 256 * (d + 1), :] = total[:, 512 + 256 * a : 768 + 256 * a]


def keyval_pair_kernel(place, keep, got, o0, o1, o2, o3):
    for i, out in enumerate((o0, o1, o2, o3)):
        rows = block(place[3] ^ i, 256)
        out[...] = (keep[rows, :] + got[rows, :]).astype(out.dtype)


def query_pair_kernel(place, keep, got, after, o0, o1, o2, o3):
    for i, out in enumerate((o0, o1, o2, o3)):
        a = place[6] ^ (0, 1, 1, 0)[i]
        rows = block(place[7] ^ (i >> 1), 512)
        out[...] = (keep[a, rows, :] + got[a, rows, :]).astype(out.dtype)


def query_ring_kernel(place, own, r1, r2, r3, after, q_keep, q_send):
    h = place[8]

    def total(rows):
        return own[rows, :] + r1[rows, :].astype(F32) + r2[rows, :].astype(F32) + r3[rows, :].astype(F32)

    q_keep[...] = total(block(h, 256))
    q_send[...] = total(block(h ^ 1, 256)).astype(BF)


def keyval_ring_kernel(place, own, r1, r2, r3, after, out):
    out[...] = (own[...] + r1[...] + r2[...] + r3[...]).astype(BF)


def keyval_lay_kernel(place, a0, a1, a2, a3, b0, b1, b2, b3, out):
    c, head = place[4], place[12]
    for half, refs in ((0, (a0, a1, a2, a3)), (1, (b0, b1, b2, b3))):
        for i, ref in enumerate(refs):
            for a in range(2):
                lanes = block(head ^ (HEAD_STEP[i] ^ (2 * a)), 128)
                out[c ^ half, :, lanes] = ref[:, 128 * a : 128 * (a + 1)]


def owner_sum_kernel(place, own, beta, side, o0, o1, o2, o3):
    for k, out in enumerate((o0, o1, o2, o3)):
        rows = slice(64 * k, 64 * (k + 1))
        out[...] = (own[rows, :] + beta[rows, :].astype(F32) + side[rows, :].astype(F32)).astype(out.dtype)


def input_grad_kernel(place, x_ref, og_ref, gain_ref, p0, p1, p2, p3, out, scaled):
    base = place[0]
    for k, ref in enumerate((p0, p1, p2, p3)):
        for j in range(4):
            lanes = block(base ^ (INNER[k] ^ OUTER[j]), 256)
            scaled[:, lanes] = ref[:, 256 * j : 256 * (j + 1)].astype(F32) * gain_ref[:, lanes]
    wide = x_ref[...].astype(F32)
    inverse = lax.rsqrt(jnp.mean(wide * wide, axis=1, keepdims=True) + EPSILON)
    unit = wide * inverse
    grad = scaled[...]
    mean_term = jnp.mean(grad * unit, axis=1, keepdims=True)
    out[...] = og_ref[...].astype(F32) + inverse * (grad - unit * mean_term)


def shards(inputs, out_grad, gain, w_query, w_keyval, grad_query, grad_keyval):
    device = lax.axis_index("dp") * 16 + lax.axis_index("tensor")
    place = lax.dynamic_index_in_dim(jnp.asarray(TABLE), device, 0, keepdims=False)
    gain_row = gain.reshape(1, 4096)

    *inner, k0, k1, k2 = call(
        prepare_kernel,
        [((512, 256), BF)] * 4 + [((128, 256), BF), ((2, 128, 256), BF), ((128, 256), BF)],
        place,
        (inputs, gain_row, w_query, w_keyval),
        [
            pltpu.VMEM((64, 4096), BF),
            pltpu.VMEM((1, 4096), F32),
            pltpu.VMEM((64, 4096), BF),
            pltpu.SemaphoreType.DMA((18,)),
        ],
        spaces=[HBM] * 4,
        limit=60,
    )
    inner = [inner[0]] + [exchange(inner[k], "tensor", INNER[k]) for k in (1, 2, 3)]
    k1 = exchange(k1, "tensor", 2)
    g1, g2 = exchange(grad_query, "tensor", 1), exchange(grad_query, "tensor", 4)
    g = (grad_query, g1, g2, exchange(g1, "tensor", 4))
    n0, k23, gkv = call(
        gather_rows_kernel,
        [((256, 1024), BF), ((2, 128, 256), BF), ((2, 1024, 128), BF)],
        place,
        (*inner, k1, k2, grad_keyval),
        [pltpu.SemaphoreType.DMA],
        spaces=[VMEM] * 6 + [HBM],
    )
    k23 = exchange(k23, "tensor", 12)
    n1 = exchange(n0, "tensor", 2)
    n = (n0, n1, exchange(n0, "tensor", 12), exchange(n1, "tensor", 12))
    (w0,) = call(
        gather_weights_kernel,
        [((4, 384, 256), BF)],
        place,
        (*inner, k0, k1, k23, g2),
        spaces=[VMEM] * 7 + [ANY],

    )
    (kv_own,) = call(
        near_kernel,
        [((2, 1024, 128), BF)],
        place,
        (gkv, exchange(gkv, "tensor", 1), w0, n1, n[2]),
        spaces=[VMEM] * 2 + [ANY] * 3,
    )
    kv_far = exchange(kv_own, "tensor", 4)
    (half,) = call(
        weight_lay_kernel,
        [((4, 128, 1536), BF)],
        place,
        (w0, exchange(w0, "dp", 4), kv_far, g1, n[3]),
        spaces=[VMEM] * 2 + [ANY] * 3,
    )
    (w,) = call(weight_join_kernel, [((4, 256, 1536), BF)], place, (half, exchange(half, "dp", 1)))

    kv_keep, kv_send = call(
        keyval_grad_kernel,
        [((1024, 256), F32)] * 2,
        place,
        (*n, kv_own, kv_far, half),
        [pltpu.VMEM((1024, 512), BF)],
        spaces=[VMEM] * 6 + [ANY],
    )

    kv = call(
        keyval_pair_kernel,
        [((256, 256), F32)] * 4,
        place,
        (kv_keep, exchange(kv_send, "dp", 1)),
    )

    def rows_grad(which, kind, after):
        return call(
            lambda *refs: rows_grad_kernel(which, *refs),
            [((256, 1024), kind)] * 2,
            place,
            (*g, kv_own, kv_far, w, after),
            [pltpu.VMEM((256, 1536), BF)],
            spaces=[VMEM] * 7 + [ANY],
        )

    kv_got = [exchange(kv[i], "dp", 4 * i) for i in (1, 2, 3)]
    both, beta = rows_grad((3, 2), BF, kv_got[0])
    both_got = exchange(both, "tensor", 12)
    beta_got = exchange(beta, "tensor", 12)
    q_keep, q_send = call(
        query_grad_kernel,
        [((2, 1024, 256), F32)] * 2,
        place,
        (*n, *g, both),
        [pltpu.VMEM((1024, 1024), BF)],
        spaces=[VMEM] * 8 + [ANY],
    )
    q_got = exchange(q_send, "dp", 1)
    q = call(
        query_pair_kernel,
        [((512, 256), F32)] + [((512, 256), BF)] * 3,
        place,
        (q_keep, q_got, kv[0]),
        spaces=[VMEM] * 2 + [ANY],
    )
    side, own = rows_grad((1, 0), F32, q[0])
    side = (side + both_got.astype(F32)).astype(BF)
    side_got = exchange(side, "tensor", 2)

    everywhere = ("dp", "tensor")
    (kv,) = call(
        keyval_ring_kernel,
        [((256, 256), BF)],
        place,
        (kv[0], *kv_got, side),
        spaces=[VMEM] * 4 + [ANY],
    )
    kv = [lax.ppermute(kv, everywhere, keyval_turn(over)).astype(F32) for over in (0, 1)]
    kv = kv[0] + kv[1]
    near = [kv] + [exchange(kv, "dp", 4 * i) for i in (1, 2, 3)]
    far = [exchange(v, "dp", 1) for v in near]
    (keyval_weight_grad,) = call(keyval_lay_kernel, [((2, 256, 1024), F32)], place, (*near, *far))

    parts = call(
        owner_sum_kernel, [((64, 1024), F32)] + [((64, 1024), BF)] * 3, place, (own, beta_got, side_got)
    )
    parts = [parts[0]] + [exchange(parts[k], "tensor", INNER[k]) for k in (1, 2, 3)]
    (input_grad,) = call(
        input_grad_kernel,
        [((64, 4096), F32)],
        place,
        (inputs, out_grad, gain_row, *parts),
        [pltpu.VMEM((64, 4096), F32)],
        cost=10**11,
    )

    q_keep, q_send = call(
        query_ring_kernel,
        [((256, 256), F32), ((256, 256), BF)],
        place,
        (q[0], *(exchange(q[i], "dp", 4 * i) for i in (1, 2, 3)), parts[0]),
        spaces=[VMEM] * 4 + [ANY],
    )
    query_weight_grad = lax.ppermute(q_keep, everywhere, query_turn(0)) + lax.ppermute(
        q_send, everywhere, query_turn(1)
    ).astype(F32)
    return (input_grad, query_weight_grad, keyval_weight_grad)


def solution(mesh):
    placed = (
        P(("dp", "tensor"), None),
        P(("dp", "tensor"), None),
        P(),
        P(None, "tensor"),
        P(None, "tensor", None),
        P("dp", "tensor"),
        P(None, "dp", "tensor"),
    )
    return jax.shard_map(
        shards,
        mesh=mesh,
        in_specs=placed,
        out_specs=(P(("dp", "tensor"), None), P("dp", "tensor"), P(None, "tensor", None)),
        check_vma=False,
    )
```

```python
import numpy as np
import jax
import jax.numpy as jnp
from jax import lax
from jax.experimental import pallas as pl
from jax.experimental.pallas import tpu as pltpu
from jax.sharding import PartitionSpec as P

EPSILON = 1e-05
BF = jnp.bfloat16
F32 = jnp.float32

INNER = (0, 1, 4, 5)
OUTER = (0, 2, 12, 14)
HEAD_STEP = (0, 1, 6, 7)


def alpha_of(v):
    return (v ^ (v >> 1)) & 1


def ring_place(alpha, beta):
    return alpha ^ (3 * beta)


def place_table():
    rows = []
    for device in range(256):
        dp, t = divmod(device, 16)
        x, c = dp >> 2, dp & 1
        h = (dp >> 1) & 1
        y, z = divmod(t, 4)
        z0, z1 = z & 1, z >> 1
        base = 4 * alpha_of(y) + z0
        outer = 2 * (y >> 1) + z1
        rows.append(
            (
                base,
                t,
                outer,
                x,
                c,
                c ^ z0,
                alpha_of(x) ^ alpha_of(y),
                x >> 1,
                h,
                base ^ OUTER[2 * (x & 1)],
                2 * y + z1,
                x & 1,
                (2 * alpha_of(y)) ^ HEAD_STEP[x],
                0,
                0,
                0,
            )
        )
    return np.array(rows, np.int32)


TABLE = place_table()


def exchange(v, axis, flip):
    return lax.ppermute(v, axis, [(i, i ^ flip) for i in range(16)])


def query_turn(over):
    pairs = []
    for device in range(256):
        dp, t = divmod(device, 16)
        x, h, c = dp >> 2, (dp >> 1) & 1, dp & 1
        y, z = divmod(t, 4)
        x_to = ring_place(alpha_of(y), x >> 1)
        y_to = ring_place(alpha_of(x), y >> 1)
        z_to, c_to = (z & 2) | c, z & 1
        pairs.append((device, (x_to * 4 + (h ^ over) * 2 + c_to) * 16 + y_to * 4 + z_to))
    return pairs


def keyval_turn(over):
    pairs = []
    for device in range(256):
        dp, t = divmod(device, 16)
        x = dp >> 2
        y, z = divmod(t, 4)
        x_to = 2 * (y >> 1) + (z >> 1)
        y_to = ring_place(alpha_of(y), x >> 1)
        z_to = 2 * (x & 1) + (z & 1)
        pairs.append((device, (x_to * 4 + ((dp & 3) ^ (2 * over))) * 16 + y_to * 4 + z_to))
    return pairs


COST = {
    "owner_sum_kernel": 4 * 10**9,
    "input_grad_kernel": 6 * 10**9,
    "keyval_lay_kernel": 6 * 10**9,
    "side_kernel": 20 * 10**9,
    "rows1": 4 * 10**9,
}

SMEM = pl.BlockSpec(memory_space=pltpu.SMEM)
VMEM = pl.BlockSpec(memory_space=pltpu.VMEM)
ANY = pl.BlockSpec(memory_space=pl.ANY)
HBM = pl.BlockSpec(memory_space=pltpu.HBM)


def call(kernel, outs, place, args, scratch=(), spaces=None, limit=40, cost=None):
    return pl.pallas_call(
        kernel,
        out_shape=[jax.ShapeDtypeStruct(s, d) for s, d in outs],
        in_specs=[SMEM] + list(spaces or [VMEM] * len(args)),
        out_specs=[VMEM] * len(outs),
        scratch_shapes=list(scratch),
        compiler_params=pltpu.CompilerParams(vmem_limit_bytes=limit << 20),
        cost_estimate=pl.CostEstimate(
            flops=COST.get(kernel.__name__, 0) if cost is None else cost, bytes_accessed=1, transcendentals=0
        ),
    )(place, *args)


def block(index, size):
    return pl.ds(pl.multiple_of(index * size, size), size)


def prepare_kernel(place, x_any, gain_any, wq, wkv, *refs):
    inner, k0, k1, k2, x_ref, gain_ref, scr, sem = refs[:4], *refs[4:]
    base, c = place[0], place[4]
    first = [
        pltpu.make_async_copy(x_any, x_ref, sem.at[0]),
        pltpu.make_async_copy(gain_any, gain_ref, sem.at[1]),
    ]
    copies = []
    for k in range(4):
        for m in range(2):
            rows = block(2 * (place[9] ^ (INNER[k] ^ OUTER[m])) + c, 128)
            to = inner[k].at[256 + 128 * m : 384 + 128 * m, :]
            copies.append(pltpu.make_async_copy(wq.at[rows, :], to, sem.at[2 + 2 * k + m]))
    for j, out in enumerate((k0, k1.at[0], k2, k1.at[1])):
        for a in range(2):
            head = block(place[10] ^ (HEAD_STEP[j] ^ (2 * a)), 128)
            to = out.at[:, 128 * a : 128 * (a + 1)]
            copies.append(pltpu.make_async_copy(wkv.at[place[11], block(c, 128), head], to, sem.at[10 + 2 * j + a]))
    for copy in first + copies:
        copy.start()
    for copy in first:
        copy.wait()
    wide = x_ref[...].astype(F32)
    inverse = lax.rsqrt(jnp.mean(wide * wide, axis=1, keepdims=True) + EPSILON)
    scr[...] = ((wide * inverse) * gain_ref[...]).astype(BF)
    for k in range(4):
        for j in range(4):
            inner[k][64 * j : 64 * (j + 1), :] = scr[:, block(base ^ (INNER[k] ^ OUTER[j]), 256)]
    for copy in copies:
        copy.wait()


def gather_rows_kernel(place, m0, m1, m2, m3, k1, k2, gkv, n, k23, gkv_out, sem):
    copy = pltpu.make_async_copy(gkv, gkv_out, sem)
    copy.start()
    for k, ref in enumerate((m0, m1, m2, m3)):
        for j in range(4):
            n[64 * k : 64 * (k + 1), 256 * j : 256 * (j + 1)] = ref[64 * j : 64 * (j + 1), :]
    k23[0] = k2[...]
    k23[1] = k1[1]
    copy.wait()


def gather_weights_kernel(place, m0, m1, m2, m3, k0, k1, k23, after, w):
    for k, ref in enumerate((m0, m1, m2, m3)):
        w[k, :256, :] = ref[256:, :]
    for j, piece in enumerate((k0[...], k1[0], k23[0], k23[1])):
        w[j, 256:, :] = piece


def near_kernel(place, own, got, a0, a1, a2, out):
    out[...] = (own[...].astype(F32) + got[...].astype(F32)).astype(BF)


def weight_lay_kernel(place, w0, w1, a0, a1, a2, out):
    outer = place[2]
    for i, ref in enumerate((w0, w1)):
        part = place[11] ^ i
        for k in range(4):
            for m in range(2):
                out[2 * part + m, :, 256 * k : 256 * (k + 1)] = ref[k, 128 * m : 128 * (m + 1), :]
                lanes = pl.ds(pl.multiple_of(1024 + 256 * m + 128 * part, 128), 128)
                out[outer ^ k, :, lanes] = ref[k, 256:, 128 * m : 128 * (m + 1)]


def weight_join_kernel(place, mine, other, out):
    c = place[4]
    for half, ref in ((0, mine), (1, other)):
        for d in range(4):
            out[d, block(c ^ half, 128), :] = ref[d]


def rows_grad_kernel(which, place, g0, g1, g2, g3, kv0, kv1, w, after, out, scr):
    t = place[1]
    for at, j in enumerate(which):
        for k in range(4):
            rows = block(t ^ (OUTER[j] ^ INNER[k]), 64)
            here = slice(64 * k, 64 * (k + 1))
            for n, g in enumerate((g0, g1, g2, g3)):
                scr[here, 256 * n : 256 * (n + 1)] = g[rows, :]
            for a, kv in enumerate((kv0, kv1)):
                for p in range(2):
                    lane = 1024 + 128 * (2 * a + p)
                    scr[here, lane : lane + 128] = kv[p, rows, :]
        left = scr[...]
        for d in range(4):
            value = lax.dot_general(left, w[d], (((1,), (1,)), ((), ())), preferred_element_type=F32)
            out[256 * at : 256 * (at + 1), 256 * d : 256 * (d + 1)] = value.astype(out.dtype)


def side_kernel(place, mine, got, after, out):
    out[...] = (mine[:256, :] + got[:256, :].astype(F32)).astype(BF)


def rows_product(ns, d, right):
    total = None
    for j, n in enumerate(ns):
        value = lax.dot_general(
            n[:, 256 * d : 256 * (d + 1)],
            right[256 * j : 256 * (j + 1), :],
            (((0,), (0,)), ((), ())),
            preferred_element_type=F32,
        )
        total = value if total is None else total + value
    return total


def keyval_grad_kernel(place, n0, n1, n2, n3, kv0, kv1, after, keep, send, right):
    t, c = place[1], place[4]
    for j in range(4):
        for k in range(4):
            rows = block(t ^ (OUTER[j] ^ INNER[k]), 64)
            here = slice(256 * j + 64 * k, 256 * j + 64 * (k + 1))
            for half in range(2):
                for a, kv in enumerate((kv0, kv1)):
                    at = 256 * half + 128 * a
                    right[here, at : at + 128] = kv[c ^ half, rows, :]
    for d in range(4):
        total = rows_product((n0, n1, n2, n3), d, right)
        keep[256 * d : 256 * (d + 1), :] = total[:, :256]
        send[256 * d : 256 * (d + 1), :] = total[:, 256:]


def query_grad_kernel(place, n0, n1, n2, n3, g0, g1, g2, g3, after, keep, send, right):
    t = place[1]
    flip = place[5] == 1
    for j in range(4):
        for k in range(4):
            rows = block(t ^ (OUTER[j] ^ INNER[k]), 64)
            here = slice(256 * j + 64 * k, 256 * j + 64 * (k + 1))
            for a, (near, far) in enumerate(((g0, g1), (g2, g3))):
                right[here, 256 * a : 256 * (a + 1)] = jnp.where(flip, far[rows, :], near[rows, :])
                right[here, 512 + 256 * a : 768 + 256 * a] = jnp.where(flip, near[rows, :], far[rows, :])
    for d in range(4):
        total = rows_product((n0, n1, n2, n3), d, right)
        for a in range(2):
            keep[a, 256 * d : 256 * (d + 1), :] = total[:, 256 * a : 256 * (a + 1)]
            send[a, 256 * d : 256 * (d + 1), :] = total[:, 512 + 256 * a : 768 + 256 * a]


def keyval_pair_kernel(place, keep, got, o0, o1, o2, o3):
    for i, out in enumerate((o0, o1, o2, o3)):
        rows = block(place[3] ^ i, 256)
        out[...] = (keep[rows, :] + got[rows, :]).astype(out.dtype)


def query_pair_kernel(place, keep, got, after, o0, o1, o2, o3):
    for i, out in enumerate((o0, o1, o2, o3)):
        a = place[6] ^ (0, 1, 1, 0)[i]
        rows = block(place[7] ^ (i >> 1), 512)
        out[...] = (keep[a, rows, :] + got[a, rows, :]).astype(out.dtype)


def query_ring_kernel(place, own, r1, r2, r3, q_keep, q_send):
    h = place[8]

    def total(rows):
        return own[rows, :] + r1[rows, :].astype(F32) + r2[rows, :].astype(F32) + r3[rows, :].astype(F32)

    q_keep[...] = total(block(h, 256))
    q_send[...] = total(block(h ^ 1, 256)).astype(BF)


def keyval_ring_kernel(place, own, r1, r2, r3, out):
    out[...] = (own[...] + r1[...] + r2[...] + r3[...]).astype(BF)


def stack_kernel(place, a0, a1, a2, a3, after, later, out):
    for i, ref in enumerate((a0, a1, a2, a3)):
        out[i] = ref[...]


def keyval_lay_kernel(place, near, far, out):
    c, head = place[4], place[12]
    for half, ref in ((0, near), (1, far)):
        for i in range(4):
            for a in range(2):
                lanes = block(head ^ (HEAD_STEP[i] ^ (2 * a)), 128)
                out[c ^ half, :, lanes] = ref[i, :, 128 * a : 128 * (a + 1)]


def owner_sum_kernel(place, mine, far, side, o0, o1, o2, o3):
    for k, out in enumerate((o0, o1, o2, o3)):
        rows, own = slice(64 * k, 64 * (k + 1)), slice(256 + 64 * k, 256 + 64 * (k + 1))
        out[...] = (mine[own, :] + far[own, :].astype(F32) + side[rows, :].astype(F32)).astype(out.dtype)


def input_grad_kernel(place, x_ref, og_ref, gain_ref, p0, p1, p2, p3, out, scaled):
    base = place[0]
    for k, ref in enumerate((p0, p1, p2, p3)):
        for j in range(4):
            lanes = block(base ^ (INNER[k] ^ OUTER[j]), 256)
            scaled[:, lanes] = ref[:, 256 * j : 256 * (j + 1)].astype(F32) * gain_ref[:, lanes]
    wide = x_ref[...].astype(F32)
    inverse = lax.rsqrt(jnp.mean(wide * wide, axis=1, keepdims=True) + EPSILON)
    unit = wide * inverse
    grad = scaled[...]
    mean_term = jnp.mean(grad * unit, axis=1, keepdims=True)
    out[...] = og_ref[...].astype(F32) + inverse * (grad - unit * mean_term)


def shards(inputs, out_grad, gain, w_query, w_keyval, grad_query, grad_keyval):
    device = lax.axis_index("dp") * 16 + lax.axis_index("tensor")
    place = lax.dynamic_index_in_dim(jnp.asarray(TABLE), device, 0, keepdims=False)
    gain_row = gain.reshape(1, 4096)

    *inner, k0, k1, k2 = call(
        prepare_kernel,
        [((512, 256), BF)] * 4 + [((128, 256), BF), ((2, 128, 256), BF), ((128, 256), BF)],
        place,
        (inputs, gain_row, w_query, w_keyval),
        [
            pltpu.VMEM((64, 4096), BF),
            pltpu.VMEM((1, 4096), F32),
            pltpu.VMEM((64, 4096), BF),
            pltpu.SemaphoreType.DMA((18,)),
        ],
        spaces=[HBM] * 4,
        limit=60,
    )
    inner = [inner[0]] + [exchange(inner[k], "tensor", INNER[k]) for k in (1, 2, 3)]
    k1 = exchange(k1, "tensor", 2)
    g1, g2 = exchange(grad_query, "tensor", 1), exchange(grad_query, "tensor", 4)
    g = (grad_query, g1, g2, exchange(g1, "tensor", 4))
    n0, k23, gkv = call(
        gather_rows_kernel,
        [((256, 1024), BF), ((2, 128, 256), BF), ((2, 1024, 128), BF)],
        place,
        (*inner, k1, k2, grad_keyval),
        [pltpu.SemaphoreType.DMA],
        spaces=[VMEM] * 6 + [HBM],
    )
    k23 = exchange(k23, "tensor", 12)
    n1 = exchange(n0, "tensor", 2)
    n = (n0, n1, exchange(n0, "tensor", 12), exchange(n1, "tensor", 12))
    (w0,) = call(
        gather_weights_kernel,
        [((4, 384, 256), BF)],
        place,
        (*inner, k0, k1, k23, g2),
        spaces=[VMEM] * 7 + [ANY],

    )
    (kv_own,) = call(
        near_kernel,
        [((2, 1024, 128), BF)],
        place,
        (gkv, exchange(gkv, "tensor", 1), w0, n1, n[2]),
        spaces=[VMEM] * 2 + [ANY] * 3,
    )
    kv_far = exchange(kv_own, "tensor", 4)
    (half,) = call(
        weight_lay_kernel,
        [((4, 128, 1536), BF)],
        place,
        (w0, exchange(w0, "dp", 4), kv_far, g1, n[3]),
        spaces=[VMEM] * 2 + [ANY] * 3,
    )
    (w,) = call(weight_join_kernel, [((4, 256, 1536), BF)], place, (half, exchange(half, "dp", 1)))

    kv_keep, kv_send = call(
        keyval_grad_kernel,
        [((1024, 256), F32)] * 2,
        place,
        (*n, kv_own, kv_far, half),
        [pltpu.VMEM((1024, 512), BF)],
        spaces=[VMEM] * 6 + [ANY],
    )

    kv = call(
        keyval_pair_kernel,
        [((256, 256), F32)] * 4,
        place,
        (kv_keep, exchange(kv_send, "dp", 1)),
    )

    def rows_grad(which, kind, after):
        return call(
            lambda *refs: rows_grad_kernel(which, *refs),
            [((512, 1024), kind)],
            place,
            (*g, kv_own, kv_far, w, after),
            [pltpu.VMEM((256, 1536), BF)],
            spaces=[VMEM] * 7 + [ANY],
            cost=COST.get("rows" + str(which[0]), 0),
        )

    kv_got = [exchange(kv[i], "dp", 4 * i) for i in (1, 2, 3)]
    (far,) = rows_grad((3, 2), BF, kv_got[0])
    far_got = exchange(far, "tensor", 12)
    q_keep, q_send = call(
        query_grad_kernel,
        [((2, 1024, 256), F32)] * 2,
        place,
        (*n, *g, far),
        [pltpu.VMEM((1024, 1024), BF)],
        spaces=[VMEM] * 8 + [ANY],
    )
    q_got = exchange(q_send, "dp", 1)
    q = call(
        query_pair_kernel,
        [((512, 256), F32)] + [((512, 256), BF)] * 3,
        place,
        (q_keep, q_got, kv[0]),
        spaces=[VMEM] * 2 + [ANY],
    )
    (mine,) = rows_grad((1, 0), F32, q[0])
    (kv_ring,) = call(
        keyval_ring_kernel,
        [((256, 256), BF)],
        place,
        (kv[0], *kv_got),
    )
    (side,) = call(side_kernel, [((256, 1024), BF)], place, (mine, far_got, kv_ring), spaces=[VMEM] * 2 + [ANY])
    side_got = exchange(side, "tensor", 2)

    everywhere = ("dp", "tensor")
    kv = [lax.ppermute(kv_ring, everywhere, keyval_turn(over)).astype(F32) for over in (0, 1)]
    kv = kv[0] + kv[1]
    near = [kv] + [exchange(kv, "dp", 4 * i) for i in (1, 2, 3)]
    parts = call(
        owner_sum_kernel, [((64, 1024), F32)] + [((64, 1024), BF)] * 3, place, (mine, far_got, side_got)
    )
    pieces = [parts[0]] + [exchange(parts[k], "tensor", INNER[k]) for k in (1, 2, 3)]
    (input_grad,) = call(
        input_grad_kernel,
        [((64, 4096), F32)],
        place,
        (inputs, out_grad, gain_row, *pieces),
        [pltpu.VMEM((64, 4096), F32)],
    )

    q_keep, q_send = call(
        query_ring_kernel,
        [((256, 256), F32), ((256, 256), BF)],
        place,
        (q[0], *(exchange(q[i], "dp", 4 * i) for i in (1, 2, 3))),
    )
    query_weight_grad = lax.ppermute(q_keep, everywhere, query_turn(0)) + lax.ppermute(
        q_send, everywhere, query_turn(1)
    ).astype(F32)
    (near,) = call(stack_kernel, [((4, 256, 256), F32)], place, (*near, q_keep, q_keep), spaces=[VMEM] * 4 + [ANY] * 2)
    (keyval_weight_grad,) = call(
        keyval_lay_kernel, [((2, 256, 1024), F32)], place, (near, exchange(near, "dp", 1))
    )
    return (input_grad, query_weight_grad, keyval_weight_grad)


def solution(mesh):
    placed = (
        P(("dp", "tensor"), None),
        P(("dp", "tensor"), None),
        P(),
        P(None, "tensor"),
        P(None, "tensor", None),
        P("dp", "tensor"),
        P(None, "dp", "tensor"),
    )
    return jax.shard_map(
        shards,
        mesh=mesh,
        in_specs=placed,
        out_specs=(P(("dp", "tensor"), None), P("dp", "tensor"), P(None, "tensor", None)),
        check_vma=False,
    )
```

```python
import numpy as np
import jax
import jax.numpy as jnp
from jax import lax
from jax.experimental import pallas as pl
from jax.experimental.pallas import tpu as pltpu
from jax.sharding import PartitionSpec as P

EPSILON = 1e-05
BF = jnp.bfloat16
F32 = jnp.float32

INNER = (0, 1, 4, 5)
OUTER = (0, 2, 12, 14)
HEAD_STEP = (0, 1, 6, 7)


def alpha_of(v):
    return (v ^ (v >> 1)) & 1


def ring_place(alpha, beta):
    return alpha ^ (3 * beta)


def place_table():
    rows = []
    for device in range(256):
        dp, t = divmod(device, 16)
        x, c = dp >> 2, dp & 1
        h = (dp >> 1) & 1
        y, z = divmod(t, 4)
        z0, z1 = z & 1, z >> 1
        base = 4 * alpha_of(y) + z0
        outer = 2 * (y >> 1) + z1
        rows.append(
            (
                base,
                t,
                outer,
                x,
                c,
                c ^ z0,
                alpha_of(x) ^ alpha_of(y),
                x >> 1,
                h,
                base ^ OUTER[2 * (x & 1)],
                2 * y + z1,
                x & 1,
                (2 * alpha_of(y)) ^ HEAD_STEP[x],
                0,
                0,
                0,
            )
        )
    return np.array(rows, np.int32)


TABLE = place_table()


def exchange(v, axis, flip):
    return lax.ppermute(v, axis, [(i, i ^ flip) for i in range(16)])


def query_turn(over):
    pairs = []
    for device in range(256):
        dp, t = divmod(device, 16)
        x, h, c = dp >> 2, (dp >> 1) & 1, dp & 1
        y, z = divmod(t, 4)
        x_to = ring_place(alpha_of(y), x >> 1)
        y_to = ring_place(alpha_of(x), y >> 1)
        z_to, c_to = (z & 2) | c, z & 1
        pairs.append((device, (x_to * 4 + (h ^ over) * 2 + c_to) * 16 + y_to * 4 + z_to))
    return pairs


def keyval_turn(over):
    pairs = []
    for device in range(256):
        dp, t = divmod(device, 16)
        x = dp >> 2
        y, z = divmod(t, 4)
        x_to = 2 * (y >> 1) + (z >> 1)
        y_to = ring_place(alpha_of(y), x >> 1)
        z_to = 2 * (x & 1) + (z & 1)
        pairs.append((device, (x_to * 4 + ((dp & 3) ^ (2 * over))) * 16 + y_to * 4 + z_to))
    return pairs


COST = {
    "owner_sum_kernel": 4 * 10**9,
    "input_grad_kernel": 6 * 10**9,
    "keyval_lay_kernel": 6 * 10**9,
    "side_kernel": 20 * 10**9,
    "rows1": 4 * 10**9,
    "keyval_ring_kernel": 10**11,
    "turn_sum_kernel": 10**11,
    "keyval_pair_kernel": 20 * 10**9,
}

SMEM = pl.BlockSpec(memory_space=pltpu.SMEM)
VMEM = pl.BlockSpec(memory_space=pltpu.VMEM)
ANY = pl.BlockSpec(memory_space=pl.ANY)
HBM = pl.BlockSpec(memory_space=pltpu.HBM)


def call(kernel, outs, place, args, scratch=(), spaces=None, limit=40, cost=None):
    return pl.pallas_call(
        kernel,
        out_shape=[jax.ShapeDtypeStruct(s, d) for s, d in outs],
        in_specs=[SMEM] + list(spaces or [VMEM] * len(args)),
        out_specs=[VMEM] * len(outs),
        scratch_shapes=list(scratch),
        compiler_params=pltpu.CompilerParams(vmem_limit_bytes=limit << 20),
        cost_estimate=pl.CostEstimate(
            flops=COST.get(kernel.__name__, 0) if cost is None else cost, bytes_accessed=1, transcendentals=0
        ),
    )(place, *args)


def block(index, size):
    return pl.ds(pl.multiple_of(index * size, size), size)


def prepare_kernel(place, x_any, gain_any, wq, wkv, *refs):
    inner, k0, k1, k2, x_ref, gain_ref, scr, sem = refs[:4], *refs[4:]
    base, c = place[0], place[4]
    first = [
        pltpu.make_async_copy(x_any, x_ref, sem.at[0]),
        pltpu.make_async_copy(gain_any, gain_ref, sem.at[1]),
    ]
    copies = []
    for k in range(4):
        for m in range(2):
            rows = block(2 * (place[9] ^ (INNER[k] ^ OUTER[m])) + c, 128)
            to = inner[k].at[256 + 128 * m : 384 + 128 * m, :]
            copies.append(pltpu.make_async_copy(wq.at[rows, :], to, sem.at[2 + 2 * k + m]))
    for j, out in enumerate((k0, k1.at[0], k2, k1.at[1])):
        for a in range(2):
            head = block(place[10] ^ (HEAD_STEP[j] ^ (2 * a)), 128)
            to = out.at[:, 128 * a : 128 * (a + 1)]
            copies.append(pltpu.make_async_copy(wkv.at[place[11], block(c, 128), head], to, sem.at[10 + 2 * j + a]))
    for copy in first + copies:
        copy.start()
    for copy in first:
        copy.wait()
    wide = x_ref[...].astype(F32)
    inverse = lax.rsqrt(jnp.mean(wide * wide, axis=1, keepdims=True) + EPSILON)
    scr[...] = ((wide * inverse) * gain_ref[...]).astype(BF)
    for k in range(4):
        for j in range(4):
            inner[k][64 * j : 64 * (j + 1), :] = scr[:, block(base ^ (INNER[k] ^ OUTER[j]), 256)]
    for copy in copies:
        copy.wait()


def gather_rows_kernel(place, m0, m1, m2, m3, k1, k2, gkv, n, k23, gkv_out, sem):
    copy = pltpu.make_async_copy(gkv, gkv_out, sem)
    copy.start()
    for k, ref in enumerate((m0, m1, m2, m3)):
        for j in range(4):
            n[64 * k : 64 * (k + 1), 256 * j : 256 * (j + 1)] = ref[64 * j : 64 * (j + 1), :]
    k23[0] = k2[...]
    k23[1] = k1[1]
    copy.wait()


def gather_weights_kernel(place, m0, m1, m2, m3, k0, k1, k23, after, w):
    for k, ref in enumerate((m0, m1, m2, m3)):
        w[k, :256, :] = ref[256:, :]
    for j, piece in enumerate((k0[...], k1[0], k23[0], k23[1])):
        w[j, 256:, :] = piece


def near_kernel(place, own, got, a0, a1, a2, out):
    out[...] = (own[...].astype(F32) + got[...].astype(F32)).astype(BF)


def weight_lay_kernel(place, w0, w1, a0, a1, a2, out):
    outer = place[2]
    for i, ref in enumerate((w0, w1)):
        part = place[11] ^ i
        for k in range(4):
            for m in range(2):
                out[2 * part + m, :, 256 * k : 256 * (k + 1)] = ref[k, 128 * m : 128 * (m + 1), :]
                lanes = pl.ds(pl.multiple_of(1024 + 256 * m + 128 * part, 128), 128)
                out[outer ^ k, :, lanes] = ref[k, 256:, 128 * m : 128 * (m + 1)]


def weight_join_kernel(place, mine, other, out):
    c = place[4]
    for half, ref in ((0, mine), (1, other)):
        for d in range(4):
            out[d, block(c ^ half, 128), :] = ref[d]


def rows_grad_kernel(which, place, g0, g1, g2, g3, kv0, kv1, w, after, out, scr):
    t = place[1]
    for at, j in enumerate(which):
        for k in range(4):
            rows = block(t ^ (OUTER[j] ^ INNER[k]), 64)
            here = slice(64 * k, 64 * (k + 1))
            for n, g in enumerate((g0, g1, g2, g3)):
                scr[here, 256 * n : 256 * (n + 1)] = g[rows, :]
            for a, kv in enumerate((kv0, kv1)):
                for p in range(2):
                    lane = 1024 + 128 * (2 * a + p)
                    scr[here, lane : lane + 128] = kv[p, rows, :]
        left = scr[...]
        for d in range(4):
            value = lax.dot_general(left, w[d], (((1,), (1,)), ((), ())), preferred_element_type=F32)
            out[256 * at : 256 * (at + 1), 256 * d : 256 * (d + 1)] = value.astype(out.dtype)


def side_kernel(place, mine, got, after, out):
    out[...] = (mine[:256, :] + got[:256, :].astype(F32)).astype(BF)


def rows_product(ns, d, right):
    total = None
    for j, n in enumerate(ns):
        value = lax.dot_general(
            n[:, 256 * d : 256 * (d + 1)],
            right[256 * j : 256 * (j + 1), :],
            (((0,), (0,)), ((), ())),
            preferred_element_type=F32,
        )
        total = value if total is None else total + value
    return total


def keyval_grad_kernel(place, n0, n1, n2, n3, kv0, kv1, after, keep, send, right):
    t, c = place[1], place[4]
    for j in range(4):
        for k in range(4):
            rows = block(t ^ (OUTER[j] ^ INNER[k]), 64)
            here = slice(256 * j + 64 * k, 256 * j + 64 * (k + 1))
            for half in range(2):
                for a, kv in enumerate((kv0, kv1)):
                    at = 256 * half + 128 * a
                    right[here, at : at + 128] = kv[c ^ half, rows, :]
    for d in range(4):
        total = rows_product((n0, n1, n2, n3), d, right)
        keep[256 * d : 256 * (d + 1), :] = total[:, :256]
        send[256 * d : 256 * (d + 1), :] = total[:, 256:]


def query_grad_kernel(place, n0, n1, n2, n3, g0, g1, g2, g3, after, keep, send, right):
    t = place[1]
    flip = place[5] == 1
    for j in range(4):
        for k in range(4):
            rows = block(t ^ (OUTER[j] ^ INNER[k]), 64)
            here = slice(256 * j + 64 * k, 256 * j + 64 * (k + 1))
            for a, (near, far) in enumerate(((g0, g1), (g2, g3))):
                right[here, 256 * a : 256 * (a + 1)] = jnp.where(flip, far[rows, :], near[rows, :])
                right[here, 512 + 256 * a : 768 + 256 * a] = jnp.where(flip, near[rows, :], far[rows, :])
    for d in range(4):
        total = rows_product((n0, n1, n2, n3), d, right)
        for a in range(2):
            keep[a, 256 * d : 256 * (d + 1), :] = total[:, 256 * a : 256 * (a + 1)]
            send[a, 256 * d : 256 * (d + 1), :] = total[:, 512 + 256 * a : 768 + 256 * a]


def keyval_pair_kernel(place, keep, got, o0, o1, o2, o3):
    for i, out in enumerate((o0, o1, o2, o3)):
        rows = block(place[3] ^ i, 256)
        out[...] = (keep[rows, :] + got[rows, :]).astype(out.dtype)


def query_pair_kernel(place, keep, got, after, o0, o1, o2, o3):
    for i, out in enumerate((o0, o1, o2, o3)):
        a = place[6] ^ (0, 1, 1, 0)[i]
        rows = block(place[7] ^ (i >> 1), 512)
        out[...] = (keep[a, rows, :] + got[a, rows, :]).astype(out.dtype)


def query_ring_kernel(place, own, r1, r2, r3, q_keep, q_send):
    h = place[8]

    def total(rows):
        return own[rows, :] + r1[rows, :].astype(F32) + r2[rows, :].astype(F32) + r3[rows, :].astype(F32)

    q_keep[...] = total(block(h, 256))
    q_send[...] = total(block(h ^ 1, 256)).astype(BF)


def keyval_ring_kernel(place, own, r1, r2, r3, out):
    out[...] = (own[...] + r1[...] + r2[...] + r3[...]).astype(BF)


def stack_kernel(place, a0, a1, a2, a3, after, later, out):
    for i, ref in enumerate((a0, a1, a2, a3)):
        out[i] = ref[...]


def keyval_lay_kernel(place, near, far, out):
    c, head = place[4], place[12]
    for half, ref in ((0, near), (1, far)):
        for i in range(4):
            for a in range(2):
                lanes = block(head ^ (HEAD_STEP[i] ^ (2 * a)), 128)
                out[c ^ half, :, lanes] = ref[i, :, 128 * a : 128 * (a + 1)]


def owner_sum_kernel(place, mine, far, side, o0, o1, o2, o3):
    for k, out in enumerate((o0, o1, o2, o3)):
        rows, own = slice(64 * k, 64 * (k + 1)), slice(256 + 64 * k, 256 + 64 * (k + 1))
        out[...] = (mine[own, :] + far[own, :].astype(F32) + side[rows, :].astype(F32)).astype(out.dtype)


def input_grad_kernel(place, x_ref, og_ref, gain_ref, p0, p1, p2, p3, out, scaled):
    base = place[0]
    for k, ref in enumerate((p0, p1, p2, p3)):
        for j in range(4):
            lanes = block(base ^ (INNER[k] ^ OUTER[j]), 256)
            scaled[:, lanes] = ref[:, 256 * j : 256 * (j + 1)].astype(F32) * gain_ref[:, lanes]
    wide = x_ref[...].astype(F32)
    inverse = lax.rsqrt(jnp.mean(wide * wide, axis=1, keepdims=True) + EPSILON)
    unit = wide * inverse
    grad = scaled[...]
    mean_term = jnp.mean(grad * unit, axis=1, keepdims=True)
    out[...] = og_ref[...].astype(F32) + inverse * (grad - unit * mean_term)


def shards(inputs, out_grad, gain, w_query, w_keyval, grad_query, grad_keyval):
    device = lax.axis_index("dp") * 16 + lax.axis_index("tensor")
    place = lax.dynamic_index_in_dim(jnp.asarray(TABLE), device, 0, keepdims=False)
    gain_row = gain.reshape(1, 4096)

    *inner, k0, k1, k2 = call(
        prepare_kernel,
        [((512, 256), BF)] * 4 + [((128, 256), BF), ((2, 128, 256), BF), ((128, 256), BF)],
        place,
        (inputs, gain_row, w_query, w_keyval),
        [
            pltpu.VMEM((64, 4096), BF),
            pltpu.VMEM((1, 4096), F32),
            pltpu.VMEM((64, 4096), BF),
            pltpu.SemaphoreType.DMA((18,)),
        ],
        spaces=[HBM] * 4,
        limit=60,
    )
    inner = [inner[0]] + [exchange(inner[k], "tensor", INNER[k]) for k in (1, 2, 3)]
    k1 = exchange(k1, "tensor", 2)
    g1, g2 = exchange(grad_query, "tensor", 1), exchange(grad_query, "tensor", 4)
    g = (grad_query, g1, g2, exchange(g1, "tensor", 4))
    n0, k23, gkv = call(
        gather_rows_kernel,
        [((256, 1024), BF), ((2, 128, 256), BF), ((2, 1024, 128), BF)],
        place,
        (*inner, k1, k2, grad_keyval),
        [pltpu.SemaphoreType.DMA],
        spaces=[VMEM] * 6 + [HBM],
    )
    k23 = exchange(k23, "tensor", 12)
    n1 = exchange(n0, "tensor", 2)
    n = (n0, n1, exchange(n0, "tensor", 12), exchange(n1, "tensor", 12))
    (w0,) = call(
        gather_weights_kernel,
        [((4, 384, 256), BF)],
        place,
        (*inner, k0, k1, k23, g2),
        spaces=[VMEM] * 7 + [ANY],

    )
    (kv_own,) = call(
        near_kernel,
        [((2, 1024, 128), BF)],
        place,
        (gkv, exchange(gkv, "tensor", 1), w0, n1, n[2]),
        spaces=[VMEM] * 2 + [ANY] * 3,
    )
    kv_far = exchange(kv_own, "tensor", 4)
    (half,) = call(
        weight_lay_kernel,
        [((4, 128, 1536), BF)],
        place,
        (w0, exchange(w0, "dp", 4), kv_far, g1, n[3]),
        spaces=[VMEM] * 2 + [ANY] * 3,
    )
    (w,) = call(weight_join_kernel, [((4, 256, 1536), BF)], place, (half, exchange(half, "dp", 1)))

    kv_keep, kv_send = call(
        keyval_grad_kernel,
        [((1024, 256), F32)] * 2,
        place,
        (*n, kv_own, kv_far, half),
        [pltpu.VMEM((1024, 512), BF)],
        spaces=[VMEM] * 6 + [ANY],
    )

    kv = call(
        keyval_pair_kernel,
        [((256, 256), F32)] * 4,
        place,
        (kv_keep, exchange(kv_send, "dp", 1)),
    )

    def rows_grad(which, kind, after):
        return call(
            lambda *refs: rows_grad_kernel(which, *refs),
            [((512, 1024), kind)],
            place,
            (*g, kv_own, kv_far, w, after),
            [pltpu.VMEM((256, 1536), BF)],
            spaces=[VMEM] * 7 + [ANY],
            cost=COST.get("rows" + str(which[0]), 0),
        )

    kv_got = [exchange(kv[i], "dp", 4 * i) for i in (1, 2, 3)]
    (far,) = rows_grad((3, 2), BF, kv_got[0])
    far_got = exchange(far, "tensor", 12)
    q_keep, q_send = call(
        query_grad_kernel,
        [((2, 1024, 256), F32)] * 2,
        place,
        (*n, *g, far),
        [pltpu.VMEM((1024, 1024), BF)],
        spaces=[VMEM] * 8 + [ANY],
    )
    q_got = exchange(q_send, "dp", 1)
    q = call(
        query_pair_kernel,
        [((512, 256), F32)] + [((512, 256), BF)] * 3,
        place,
        (q_keep, q_got, kv[0]),
        spaces=[VMEM] * 2 + [ANY],
    )
    (mine,) = rows_grad((1, 0), F32, q[0])
    (kv_ring,) = call(
        keyval_ring_kernel,
        [((256, 256), BF)],
        place,
        (kv[0], *kv_got),
    )
    (side,) = call(side_kernel, [((256, 1024), BF)], place, (mine, far_got, kv_ring), spaces=[VMEM] * 2 + [ANY])
    side_got = exchange(side, "tensor", 2)

    everywhere = ("dp", "tensor")
    kv = [lax.ppermute(kv_ring, everywhere, keyval_turn(over)).astype(F32) for over in (0, 1)]
    kv = kv[0] + kv[1]
    near = [kv] + [exchange(kv, "dp", 4 * i) for i in (1, 2, 3)]
    parts = call(
        owner_sum_kernel, [((64, 1024), F32)] + [((64, 1024), BF)] * 3, place, (mine, far_got, side_got)
    )
    pieces = [parts[0]] + [exchange(parts[k], "tensor", INNER[k]) for k in (1, 2, 3)]
    (input_grad,) = call(
        input_grad_kernel,
        [((64, 4096), F32)],
        place,
        (inputs, out_grad, gain_row, *pieces),
        [pltpu.VMEM((64, 4096), F32)],
    )

    q_keep, q_send = call(
        query_ring_kernel,
        [((256, 256), F32), ((256, 256), BF)],
        place,
        (q[0], *(exchange(q[i], "dp", 4 * i) for i in (1, 2, 3))),
    )
    query_weight_grad = lax.ppermute(q_keep, everywhere, query_turn(0)) + lax.ppermute(
        q_send, everywhere, query_turn(1)
    ).astype(F32)
    (near,) = call(stack_kernel, [((4, 256, 256), F32)], place, (*near, q_keep, q_keep), spaces=[VMEM] * 4 + [ANY] * 2)
    (keyval_weight_grad,) = call(
        keyval_lay_kernel, [((2, 256, 1024), F32)], place, (near, exchange(near, "dp", 1))
    )
    return (input_grad, query_weight_grad, keyval_weight_grad)


def solution(mesh):
    placed = (
        P(("dp", "tensor"), None),
        P(("dp", "tensor"), None),
        P(),
        P(None, "tensor"),
        P(None, "tensor", None),
        P("dp", "tensor"),
        P(None, "dp", "tensor"),
    )
    return jax.shard_map(
        shards,
        mesh=mesh,
        in_specs=placed,
        out_specs=(P(("dp", "tensor"), None), P("dp", "tensor"), P(None, "tensor", None)),
        check_vma=False,
    )
```
